512 devices in a mesh: rep: 16 (over y, x_lo), fsdp: 8 (over z), tp: 4 (over x_hi, core).
Axes of the slice: x: 4 (x_hi: 2, x_lo: 2; x = x_hi * 2 + x_lo), y: 8, z: 8, core: 2. Of those that a mesh axis runs over, the one named last changes fastest.
Arguments:
- grad_parts: bfloat16 [8, 2, 8192, 1024], P('fsdp', None, 'rep', 'tp'), may hold values from -4 to 4
- master_weight: float32 [2, 8192, 1024], P(None, ('rep', 'fsdp'), 'tp'), may hold values from -0.0625 to 0.0625
- moment_one: float32 [2, 8192, 1024], P(None, ('rep', 'fsdp'), 'tp'), may hold values from -4 to 4
- moment_two: float32 [2, 8192, 1024], P(None, ('rep', 'fsdp'), 'tp'), may hold values from 0.1 to 2
- layer_inputs: bfloat16 [6144, 4, 8192], P(('rep', 'fsdp'), None, 'tp'), may hold values from -6 to 6
- queries: bfloat16 [6144, 4, 8192], P(('rep', 'fsdp'), None, 'tp'), may hold values from -105 to 105
- kv_cache: bfloat16 [6144, 24, 2, 1024], P(('rep', 'fsdp'), None, None, 'tp'), may hold values from -4 to 4
- lengths: int32 [6144], P(('rep', 'fsdp')), may hold values from 2 to 24
Outputs:
- new_master: float32 [2, 8192, 1024], P(None, ('rep', 'fsdp'), 'tp')
- new_moment_one: float32 [2, 8192, 1024], P(None, ('rep', 'fsdp'), 'tp')
- new_moment_two: float32 [2, 8192, 1024], P(None, ('rep', 'fsdp'), 'tp')
- context: bfloat16 [6144, 4, 8192], P(('rep', 'fsdp'), None, 'tp')
The draws below stay inside these ranges and needn't reach their ends.
Inputs may be any that keep to these rules, and one draw needn't show every extreme that they name: lengths[r] is the number of valid cached positions of row r, at most 24.
All inputs are finite; a program needn't handle non-finite values.
Results may differ from the reference program's by a relative error of at most 0.0065.
Values may be sent and summed in bfloat16 or wider, within the bound.
No kernel may reach another device: no remote copies, remote signals or barrier semaphores. Data moves between devices by JAX's collectives and lax.ppermute only.
A program may use at most 64 MiB of HBM per device.

```python
import math
import jax
import jax.numpy as jnp
from jax import lax

D = 8192
QH = 64
KVH = 8
HD = 128
ROW_DEV = 48
CACHE = 24
STEPS = 4
ROWS = 6144
KVW = 1024
N_FSDP = 8


def shared_cache(key):
    base = jax.random.normal(jax.random.fold_in(key, 11), (ROWS, CACHE, 2, KVH * HD), jnp.float32)
    base = jnp.clip(base, -4.0, 4.0)
    return base


def draw_kv_cache(key, part):
    return shared_cache(key).astype(jnp.bfloat16)


def draw_queries(key, part):
    drawn = jax.random.normal(jax.random.fold_in(key, 12), (ROWS, STEPS, QH * HD), jnp.float32)
    drawn = jnp.clip(drawn, -4.0, 4.0)
    return drawn.astype(jnp.bfloat16)


def set_ends(array, key, smallest, top_value):
    extent = array.shape
    index_at = [jax.random.randint(jax.random.fold_in(key, axis), (), 0, extent[axis]) for axis in range(len(extent))]
    array = array.at[tuple(index_at)].set(smallest)
    longest = extent.index(max(extent))
    index_at[longest] = (index_at[longest] + 1) % extent[longest]
    return array.at[tuple(index_at)].set(top_value)


def spiked(drawn, stream_key, source, target, shards_of, factor):
    owner, partner = [(jnp.arange(drawn.shape[position]) // (drawn.shape[position] // shards_of)).reshape([-1 if axis == position else 1 for axis in range(drawn.ndim)]) for position in (source, target)]
    chosen = jax.random.permutation(stream_key, shards_of)[partner]
    strong = (owner == chosen) | (owner == (partner + shards_of // 2) % shards_of)
    return jnp.where(strong, factor * drawn, drawn)


def block_scale(stream_key, dims, split, smallest, largest):
    gain, own = 1.0, jax.random.fold_in(stream_key, 6)
    for position, blocks in split:
        steps = jnp.exp(jax.random.uniform(jax.random.fold_in(own, position), (blocks,), jnp.float32, smallest / len(split), largest / len(split)))
        gain = gain * jnp.repeat(steps, dims[position] // blocks).reshape([-1 if axis == position else 1 for axis in range(len(dims))])
    return gain


def noise(key, shape, spread, bound, cuts=(), held_as=jnp.bfloat16):
    gain = block_scale(key, shape, cuts, -0.22, 0.18) if cuts else 1.0
    array = jax.random.normal(key, shape, jnp.float32) * spread * gain
    return jnp.minimum(jnp.maximum(array, -bound), bound).astype(held_as)


def bell_draw_with(key, dims, spread, most, cuts, heavy, kind=jnp.bfloat16):
    values = spread * jax.random.normal(key, dims, jnp.float32)
    if cuts:
        values = values * block_scale(key, dims, cuts, -0.22, 0.18)
    return jnp.clip(spiked(values, jax.random.fold_in(key, 3), *heavy), -most, most).astype(kind)


def setup_inputs(seed: int = 0) -> dict:
    splits = jax.random.split(jax.random.key(seed), 9)
    grad_parts = bell_draw_with(splits[0], (N_FSDP, 2, D, KVW), 0.5, 4.0, ((0, 8), (2, 16), (3, 4)), (0, 2, 8, 2.0))
    master_weight = noise(splits[1], (2, D, KVW), D ** -0.5, 0.0625, ((1, 128), (2, 4)), jnp.float32)
    moment_one = noise(splits[2], (2, D, KVW), 0.3, 4.0, ((1, 128), (2, 4)), jnp.float32)
    moment_two = jnp.clip(jnp.exp(math.log(2.0) - 2.9957323 * jax.random.uniform(splits[3], (2, D, KVW), jnp.float32) ** block_scale(splits[3], (2, D, KVW), ((1, 128), (2, 4)), -0.2, 0.2)), 0.1, 2.0)
    layer_inputs = noise(splits[4], (ROWS, STEPS, D), 1.0, 6.0, ((0, 128), (2, 4)))
    queries = draw_queries(jax.random.fold_in(splits[8], 71), 0)
    kv_cache = draw_kv_cache(jax.random.fold_in(splits[8], 71), 0)
    lengths = set_ends(jax.random.randint(splits[7], (ROWS,), 2, CACHE + 1), jax.random.fold_in(splits[7], 1), 2, CACHE).astype(jnp.int32)
    return {"grad_parts": grad_parts, "master_weight": master_weight, "moment_one": moment_one, "moment_two": moment_two, "layer_inputs": layer_inputs, "queries": queries, "kv_cache": kv_cache, "lengths": lengths}


beta_one = 0.9
beta_two = 0.95
learning_rate = 0.001
weight_decay = 0.1
epsilon = 1e-08
first_bias = 1.0 - 0.9 ** 10
second_bias = 1.0 - 0.95 ** 10

def adamw_update(gradient, master, moment_one, moment_two):
    new_one = beta_one * moment_one + (1.0 - beta_one) * gradient
    new_two = beta_two * moment_two + (1.0 - beta_two) * gradient * gradient
    update = new_one / first_bias / (jnp.sqrt(new_two / second_bias) + epsilon)
    new_master = master - learning_rate * (update + weight_decay * master)
    return (new_one, new_two, new_master)

def attend(pieces):
    query_block, cache_block, fresh_keys, fresh_values, length_block = pieces
    row_count = query_block.shape[0]
    step_count = query_block.shape[1]
    kv_heads = fresh_keys.shape[2]
    cache_len = cache_block.shape[1]
    grouped = query_block.reshape(row_count, step_count, kv_heads, -1, HD).astype(jnp.float32)
    cached_keys = cache_block[:, :, 0].reshape(row_count, cache_len, kv_heads, HD).astype(jnp.float32)
    cached_values = cache_block[:, :, 1].reshape(row_count, cache_len, kv_heads, HD).astype(jnp.float32)
    scaling = 1.0 / jnp.sqrt(jnp.float32(HD))
    cached_scores = jnp.einsum('rsgqd,rcgd->rsgqc', grouped, cached_keys) * scaling
    fresh_scores = jnp.einsum('rsgqd,rugd->rsgqu', grouped, fresh_keys.astype(jnp.float32)) * scaling
    valid_old = jnp.arange(cache_len, dtype=jnp.int32)[None, :] < length_block[:, None]
    valid_old = valid_old[:, None, None, None, :]
    steps_index = jnp.arange(step_count, dtype=jnp.int32)
    valid_new = (steps_index[None, :] <= steps_index[:, None])[None, :, None, None, :]
    scores = jnp.concatenate([jnp.where(valid_old, cached_scores, -jnp.inf), jnp.where(valid_new, fresh_scores, -jnp.inf)], axis=-1)
    row_max = lax.optimization_barrier(jnp.max(scores, axis=-1, keepdims=True))
    exponent = jnp.exp(scores - row_max)
    weights = (exponent / lax.optimization_barrier(jnp.sum(exponent, axis=-1, keepdims=True))).astype(jnp.bfloat16).astype(jnp.float32)
    output = jnp.einsum('rsgqc,rcgd->rsgqd', weights[..., :cache_len], cached_values)
    output = output + jnp.einsum('rsgqu,rugd->rsgqd', weights[..., cache_len:], fresh_values.astype(jnp.float32))
    return output.astype(jnp.bfloat16).reshape(row_count, step_count, -1)

def reference(grad_parts, master_weight, moment_one, moment_two, layer_inputs, queries, kv_cache, lengths):
    gradient = lax.optimization_barrier(jnp.sum(grad_parts.astype(jnp.float32), axis=0))
    new_one, new_two, new_master = adamw_update(gradient, master_weight, moment_one, moment_two)
    rollout_weight = new_master.astype(jnp.bfloat16)
    flattened = layer_inputs.reshape(ROWS * STEPS, D)
    fresh_keys = jnp.dot(flattened, rollout_weight[0], preferred_element_type=jnp.float32).astype(jnp.bfloat16)
    fresh_values = jnp.dot(flattened, rollout_weight[1], preferred_element_type=jnp.float32).astype(jnp.bfloat16)
    blocks = ROWS // ROW_DEV
    pieces = (queries.reshape(blocks, ROW_DEV, STEPS, QH * HD), kv_cache.reshape(blocks, ROW_DEV, CACHE, 2, KVH * HD), fresh_keys.reshape(blocks, ROW_DEV, STEPS, KVH, HD), fresh_values.reshape(blocks, ROW_DEV, STEPS, KVH, HD), lengths.reshape(blocks, ROW_DEV))
    context = lax.map(attend, pieces).reshape(ROWS, STEPS, QH * HD)
    return (new_master, new_one, new_two, context)
```

```python
import jax
import jax.numpy as jnp
from jax import lax
from jax.experimental import pallas as pl
from jax.experimental.pallas import tpu as pltpu
from jax.sharding import Mesh
from jax.sharding import PartitionSpec as P

HD = 128
ROWS = 48
STEPS = 4
TOK = ROWS * STEPS
CACHE = 24
FEAT = 2048
COLS = 256
PACK = 4
GROUPS = ROWS // PACK
AXES = ("yh", "yl", "xl", "zh", "zl", "xh", "c")
SHARD = ("yh", "yl", "xl", "zh", "zl")
REP = ("yh", "yl", "xl")
FSDP = ("zh", "zl")
TP = ("xh", "c")
CUBE = ("yl", "xl", "zl")
FAR = ("yh", "zh")

beta_one = 0.9
beta_two = 0.95
learning_rate = 0.001
weight_decay = 0.1
epsilon = 1e-08
first_bias = 1.0 - 0.9**10
second_bias = 1.0 - 0.95**10


def adamw_update(gradient, master, moment_one, moment_two):
    new_one = beta_one * moment_one + (1.0 - beta_one) * gradient
    new_two = beta_two * moment_two + (1.0 - beta_two) * gradient * gradient
    update = new_one / first_bias / (jnp.sqrt(new_two / second_bias) + epsilon)
    new_master = master - learning_rate * (update + weight_decay * master)
    return (new_one, new_two, new_master)


def split_kernel(x_ref, o_ref):
    for b in range(4):
        v = [x_ref[:, b * 512 + 128 * k : b * 512 + 128 * (k + 1)] for k in range(4)]
        for half in range(2):
            cut = slice(64 * half, 64 * (half + 1))
            for p in range(2):
                o_ref[2 * b + half, :, 128 * p : 128 * (p + 1)] = jnp.concatenate(
                    [v[2 * p][:, cut], v[2 * p + 1][:, cut]], axis=1
                )


def split_features(x):
    return pl.pallas_call(
        split_kernel,
        out_shape=jax.ShapeDtypeStruct((8, TOK, COLS), jnp.bfloat16),
        grid=(1,),
        in_specs=[pl.BlockSpec((TOK, FEAT), lambda i: (0, 0))],
        out_specs=pl.BlockSpec((8, TOK, COLS), lambda i: (0, 0, 0)),
        name="split_features",
    )(x)


def project_kernel(x_ref, w_ref, o_ref):
    for kv in range(2):
        total = None
        for j in range(4):
            w = w_ref[4 * j : 4 * j + 4, kv].reshape(COLS, COLS)
            part = jnp.dot(x_ref[j, 0], w, preferred_element_type=jnp.float32)
            total = part if total is None else total + part
        o_ref[0, :, kv * COLS : (kv + 1) * COLS] = total.astype(jnp.bfloat16)


def project(x, w):
    return pl.pallas_call(
        project_kernel,
        out_shape=jax.ShapeDtypeStruct((8, TOK, 2 * COLS), jnp.bfloat16),
        grid=(8,),
        in_specs=[
            pl.BlockSpec((4, 1, TOK, COLS), lambda i: (0, i, 0, 0)),
            pl.BlockSpec((16, 2, 64, COLS), lambda i: (0, 0, 0, 0)),
        ],
        out_specs=pl.BlockSpec((1, TOK, 2 * COLS), lambda i: (i, 0, 0)),
        name="project",
    )(x, w)


def attend_kernel(per, part_ref, q_ref, k_ref, v_ref, mask_ref, o_ref):
    width = PACK * (CACHE + STEPS)
    old = PACK * CACHE
    new = PACK * STEPS
    row = lax.broadcasted_iota(jnp.int32, (8 * new, width), 0)
    col = lax.broadcasted_iota(jnp.int32, (8 * new, width), 1)
    own = (row // STEPS) % PACK
    own_col = jnp.where(col < old, col // CACHE, (col - old) // STEPS)
    seen = (own == own_col) & ((col < old) | ((col - old) % STEPS <= row % STEPS))
    for i in range(per):
        fresh = part_ref[0, new * i : new * (i + 1), :].astype(jnp.float32)
        for j in range(1, 8):
            fresh = fresh + part_ref[j, new * i : new * (i + 1), :].astype(jnp.float32)
        fresh = fresh.astype(jnp.bfloat16)
        valid = seen & (mask_ref[0, i : i + 1, :] > 0.0)
        for g in range(2):
            lanes = slice(HD * g, HD * (g + 1))
            q = jnp.concatenate(
                [
                    q_ref[new * i : new * (i + 1), HD * (8 * g + h) : HD * (8 * g + h + 1)]
                    for h in range(8)
                ],
                axis=0,
            )
            k = jnp.concatenate([k_ref[old * i : old * (i + 1), lanes], fresh[:, lanes]], axis=0)
            v = jnp.concatenate(
                [
                    v_ref[old * i : old * (i + 1), lanes],
                    fresh[:, COLS + HD * g : COLS + HD * (g + 1)],
                ],
                axis=0,
            )
            scores = lax.dot_general(
                q, k, (((1,), (1,)), ((), ())), preferred_element_type=jnp.float32
            )
            scores = jnp.where(valid, scores * (1.0 / HD**0.5), -jnp.inf)
            top = jnp.max(scores, axis=1, keepdims=True)
            e = jnp.exp(scores - top)
            weights = (e / jnp.sum(e, axis=1, keepdims=True)).astype(jnp.bfloat16)
            out = jnp.dot(weights, v, preferred_element_type=jnp.float32).astype(jnp.bfloat16)
            for h in range(8):
                o_ref[new * i : new * (i + 1), HD * (8 * g + h) : HD * (8 * g + h + 1)] = out[
                    new * h : new * (h + 1)
                ]


def attend(parts, q, keys, values, mask, blocks=4):
    per = GROUPS // blocks
    new = PACK * STEPS * per
    old = PACK * CACHE * per
    width = PACK * (CACHE + STEPS)

    def kernel(*refs):
        attend_kernel(per, *refs)

    return pl.pallas_call(
        kernel,
        out_shape=jax.ShapeDtypeStruct((TOK, FEAT), jnp.bfloat16),
        grid=(blocks,),
        in_specs=[
            pl.BlockSpec((8, new, 2 * COLS), lambda i: (0, i, 0)),
            pl.BlockSpec((new, FEAT), lambda i: (i, 0)),
            pl.BlockSpec((old, COLS), lambda i: (i, 0)),
            pl.BlockSpec((old, COLS), lambda i: (i, 0)),
            pl.BlockSpec((1, per, width), lambda i: (i, 0, 0)),
        ],
        out_specs=pl.BlockSpec((new, FEAT), lambda i: (i, 0)),
        name="attend",
    )(parts, q, keys, values, mask.reshape(blocks, per, width))


def on_device(
    grad_parts, master_weight, moment_one, moment_two, layer_inputs, queries, kv_cache, lengths
):
    pieces = jnp.moveaxis(grad_parts[0].reshape(2, 8, 64, COLS), 1, 0)
    pieces = lax.all_to_all(pieces, FSDP, 0, 0, tiled=True)
    gradient = jnp.sum(pieces.astype(jnp.float32), axis=0)
    new_one, new_two, new_master = adamw_update(gradient, master_weight, moment_one, moment_two)
    rollout = new_master.astype(jnp.bfloat16)

    features = split_features(layer_inputs.reshape(TOK, FEAT))
    features = lax.all_to_all(features, CUBE, 0, 0, tiled=True)
    features = lax.all_gather(features, TP)

    weight = jnp.broadcast_to(rollout[None], (16, 2, 64, COLS))
    weight = lax.all_to_all(weight, FAR, 0, 0, tiled=True)

    partial = project(features, weight)
    partial = lax.all_to_all(partial, CUBE, 0, 0, tiled=True)

    keys = kv_cache[:, :, 0].reshape(ROWS * CACHE, COLS)
    values = kv_cache[:, :, 1].reshape(ROWS * CACHE, COLS)
    cached = jnp.arange(CACHE, dtype=jnp.int32)[None, :] < lengths[:, None]
    mask = jnp.concatenate(
        [
            cached.reshape(GROUPS, PACK * CACHE).astype(jnp.float32),
            jnp.ones((GROUPS, PACK * STEPS), jnp.float32),
        ],
        axis=1,
    )
    context = attend(partial, queries.reshape(TOK, FEAT), keys, values, mask)
    return (new_master, new_one, new_two, context.reshape(ROWS, STEPS, FEAT))


def solution(mesh):
    finer = Mesh(mesh.devices.reshape(4, 2, 2, 4, 2, 2, 2), AXES)
    shard = P(None, SHARD, TP)
    return jax.shard_map(
        on_device,
        mesh=finer,
        in_specs=(
            P(FSDP, None, REP, TP),
            shard,
            shard,
            shard,
            P(SHARD, None, TP),
            P(SHARD, None, TP),
            P(SHARD, None, None, TP),
            P(SHARD),
        ),
        out_specs=(shard, shard, shard, P(SHARD, None, TP)),
        check_vma=False,
    )
```

```python
import jax
import jax.numpy as jnp
from jax import lax
from jax.experimental import pallas as pl
from jax.experimental.pallas import tpu as pltpu
from jax.sharding import Mesh
from jax.sharding import PartitionSpec as P

HD = 128
ROWS = 48
STEPS = 4
TOK = ROWS * STEPS
CACHE = 24
FEAT = 2048
COLS = 256
PACK = 4
GROUPS = ROWS // PACK
AXES = ("yh", "yl", "xl", "zh", "zl", "xh", "c")
SHARD = ("yh", "yl", "xl", "zh", "zl")
REP = ("yh", "yl", "xl")
FSDP = ("zh", "zl")
TP = ("xh", "c")
CUBE = ("yl", "xl", "zl")
FAR = ("yh", "zh")

beta_one = 0.9
beta_two = 0.95
learning_rate = 0.001
weight_decay = 0.1
epsilon = 1e-08
first_bias = 1.0 - 0.9**10
second_bias = 1.0 - 0.95**10


def adamw_update(gradient, master, moment_one, moment_two):
    new_one = beta_one * moment_one + (1.0 - beta_one) * gradient
    new_two = beta_two * moment_two + (1.0 - beta_two) * gradient * gradient
    update = new_one / first_bias / (jnp.sqrt(new_two / second_bias) + epsilon)
    new_master = master - learning_rate * (update + weight_decay * master)
    return (new_one, new_two, new_master)


VM = pl.BlockSpec(memory_space=pltpu.VMEM)
SM = pl.BlockSpec(memory_space=pltpu.SMEM)
PARAMS = pltpu.CompilerParams(vmem_limit_bytes=40 << 20)


def split_kernel(x_ref, o_ref):
    for b in range(4):
        v = [
            x_ref[:, :, 512 * b + 128 * k : 512 * b + 128 * (k + 1)].reshape(TOK, 128)
            for k in range(4)
        ]
        for half in range(2):
            cut = slice(64 * half, 64 * (half + 1))
            for p in range(2):
                o_ref[2 * b + half, :, 128 * p : 128 * (p + 1)] = jnp.concatenate(
                    [v[2 * p][:, cut], v[2 * p + 1][:, cut]], axis=1
                )


def split_features(x):
    return pl.pallas_call(
        split_kernel,
        out_shape=jax.ShapeDtypeStruct((8, TOK, COLS), jnp.bfloat16),
        in_specs=[VM],
        out_specs=VM,
        compiler_params=PARAMS,
        name="split_features",
    )(x)


def project_kernel(t_ref, xa, xb, xc, xd, w_ref, o_ref):
    own = t_ref[0]
    for kv in range(2):
        w = jnp.concatenate(
            [w_ref[pl.ds(4 * (own ^ f), 4), kv].reshape(COLS, COLS) for f in range(4)], axis=0
        )
        for m in range(0, 8, 2):
            x = jnp.concatenate(
                [r[m : m + 2].reshape(2 * TOK, COLS) for r in (xa, xb, xc, xd)], axis=1
            )
            y = jnp.dot(x, w, preferred_element_type=jnp.float32).astype(jnp.bfloat16)
            o_ref[m : m + 2, :, kv * COLS : (kv + 1) * COLS] = y.reshape(2, TOK, COLS)


def project(own, features, w):
    return pl.pallas_call(
        project_kernel,
        out_shape=jax.ShapeDtypeStruct((8, TOK, 2 * COLS), jnp.bfloat16),
        in_specs=[SM] + [VM] * 5,
        out_specs=VM,
        compiler_params=PARAMS,
        name="project",
    )(own, *features, w)


def seen_bias(axis):
    width, old, count = PACK * (CACHE + STEPS), PACK * CACHE, 8 * PACK * STEPS
    shape = (count, width) if axis == 1 else (width, count)
    row = lax.broadcasted_iota(jnp.int32, shape, 1 - axis)
    col = lax.broadcasted_iota(jnp.int32, shape, axis)
    own = (row // STEPS) % PACK
    of_col = jnp.where(col < old, col // CACHE, (col - old) // STEPS)
    seen = (own == of_col) & ((col < old) | ((col - old) % STEPS <= row % STEPS))
    return jnp.where(seen, 0.0, -jnp.inf)


def attend_kernel(part_ref, q_ref, k_ref, v_ref, mask_ref, mask_t_ref, o_ref):
    old, new = PACK * CACHE, PACK * STEPS
    width, count = old + new, 8 * new
    scale = 1.4426950408889634 / HD**0.5
    base, base_t = seen_bias(1), seen_bias(0)
    eye = lax.broadcasted_iota(jnp.int32, (count, count), 0) == lax.broadcasted_iota(
        jnp.int32, (count, count), 1
    )
    minus = jnp.full((width, count), -1.0, jnp.bfloat16)
    ones = jnp.ones((width, HD), jnp.bfloat16)
    for i in range(GROUPS):
        rows = slice(PACK * i, PACK * (i + 1))
        fresh = part_ref[0, new * i : new * (i + 1), :].astype(jnp.float32)
        for j in range(1, 8):
            fresh = fresh + part_ref[j, new * i : new * (i + 1), :].astype(jnp.float32)
        fresh = fresh.astype(jnp.bfloat16)
        bias = base + mask_ref[i : i + 1, :]
        bias_t = base_t + mask_t_ref[:, i : i + 1]
        for g in range(2):
            lanes = slice(HD * g, HD * (g + 1))
            heads = [slice(HD * (8 * g + h), HD * (8 * g + h + 1)) for h in range(8)]
            q = jnp.concatenate([q_ref[rows, :, h].reshape(new, HD) for h in heads], axis=0)
            k = jnp.concatenate([k_ref[old * i : old * (i + 1), lanes], fresh[:, lanes]], axis=0)
            v = jnp.concatenate(
                [
                    v_ref[old * i : old * (i + 1), lanes],
                    fresh[:, COLS + HD * g : COLS + HD * (g + 1)],
                ],
                axis=0,
            )
            turned = lax.dot_general(
                k, q, (((1,), (1,)), ((), ())), preferred_element_type=jnp.float32
            )
            top = jnp.max(turned + bias_t, axis=0, keepdims=True)
            shift = jnp.where(eye, top, 0.0).astype(jnp.bfloat16)
            scores = lax.dot_general(
                jnp.concatenate([q, shift], axis=1),
                jnp.concatenate([k, minus], axis=1),
                (((1,), (1,)), ((), ())),
                preferred_element_type=jnp.float32,
            )
            e = jnp.exp2(scores * scale + bias).astype(jnp.bfloat16)
            out = jnp.dot(
                e, jnp.concatenate([v, ones], axis=1), preferred_element_type=jnp.float32
            )
            out = (out[:, :HD] / out[:, HD:]).astype(jnp.bfloat16)
            for n, h in enumerate(heads):
                o_ref[rows, :, h] = out[new * n : new * (n + 1)].reshape(PACK, STEPS, HD)


def attend(parts, q, keys, values, mask):
    return pl.pallas_call(
        attend_kernel,
        out_shape=jax.ShapeDtypeStruct((ROWS, STEPS, FEAT), jnp.bfloat16),
        in_specs=[VM] * 6,
        out_specs=VM,
        compiler_params=PARAMS,
        name="attend",
    )(parts, q, keys, values, mask, mask.T)


def flipped(x, axis):
    return lax.ppermute(x, axis, [(0, 1), (1, 0)])


def on_device(
    grad_parts, master_weight, moment_one, moment_two, layer_inputs, queries, kv_cache, lengths
):
    pieces = jnp.moveaxis(grad_parts[0].reshape(2, 8, 64, COLS), 1, 0)
    pieces = lax.all_to_all(pieces, FSDP, 0, 0, tiled=True)
    gradient = jnp.sum(pieces.astype(jnp.float32), axis=0)
    new_one, new_two, new_master = adamw_update(gradient, master_weight, moment_one, moment_two)
    rollout = new_master.astype(jnp.bfloat16)

    features = split_features(layer_inputs)
    features = lax.all_to_all(features, CUBE, 0, 0, tiled=True)
    beside = flipped(features, "c")
    across = flipped(features, "xh")
    beyond = flipped(across, "c")

    weight = jnp.broadcast_to(rollout[None], (16, 2, 64, COLS))
    weight = lax.all_to_all(weight, FAR, 0, 0, tiled=True)

    own = (lax.axis_index("xh") * 2 + lax.axis_index("c")).astype(jnp.int32).reshape(1)
    partial = project(own, (features, beside, across, beyond), weight)
    partial = lax.all_to_all(partial, CUBE, 0, 0, tiled=True)

    keys = kv_cache[:, :, 0].reshape(ROWS * CACHE, COLS)
    values = kv_cache[:, :, 1].reshape(ROWS * CACHE, COLS)
    cached = jnp.arange(CACHE, dtype=jnp.int32)[None, :] < lengths[:, None]
    mask = jnp.concatenate(
        [
            jnp.where(cached, 0.0, -jnp.inf).reshape(GROUPS, PACK * CACHE),
            jnp.zeros((GROUPS, PACK * STEPS), jnp.float32),
        ],
        axis=1,
    )
    context = attend(partial, queries, keys, values, mask)
    return (new_master, new_one, new_two, context)


def solution(mesh):
    finer = Mesh(mesh.devices.reshape(4, 2, 2, 4, 2, 2, 2), AXES)
    shard = P(None, SHARD, TP)
    return jax.shard_map(
        on_device,
        mesh=finer,
        in_specs=(
            P(FSDP, None, REP, TP),
            shard,
            shard,
            shard,
            P(SHARD, None, TP),
            P(SHARD, None, TP),
            P(SHARD, None, None, TP),
            P(SHARD),
        ),
        out_specs=(shard, shard, shard, P(SHARD, None, TP)),
        check_vma=False,
    )
```

```python
import jax
import jax.numpy as jnp
from jax import lax
from jax.experimental import pallas as pl
from jax.experimental.pallas import tpu as pltpu
from jax.sharding import Mesh
from jax.sharding import PartitionSpec as P

HD = 128
ROWS = 48
STEPS = 4
TOK = ROWS * STEPS
CACHE = 24
FEAT = 2048
COLS = 256
PACK = 4
GROUPS = ROWS // PACK
BATCH = 4
AXES = ("yh", "yl", "xl", "zh", "zl", "xh", "c")
SHARD = ("yh", "yl", "xl", "zh", "zl")
REP = ("yh", "yl", "xl")
FSDP = ("zh", "zl")
TP = ("xh", "c")
CUBE = ("yl", "xl", "zl")
FAR = ("yh", "zh")

beta_one = 0.9
beta_two = 0.95
learning_rate = 0.001
weight_decay = 0.1
epsilon = 1e-08
first_bias = 1.0 - 0.9**10
second_bias = 1.0 - 0.95**10


VM = pl.BlockSpec(memory_space=pltpu.VMEM)
SM = pl.BlockSpec(memory_space=pltpu.SMEM)
PARAMS = pltpu.CompilerParams(vmem_limit_bytes=40 << 20)


def by_owner_kernel(g_ref, o_ref, sems):
    copies = [
        pltpu.make_async_copy(g_ref.at[0, kv], o_ref.at[:, kv], sems.at[kv]) for kv in range(2)
    ]
    for copy in copies:
        copy.start()
    for copy in copies:
        copy.wait()


def by_owner(grads):
    return pl.pallas_call(
        by_owner_kernel,
        out_shape=jax.ShapeDtypeStruct((8, 2, 64, COLS), jnp.bfloat16),
        in_specs=[pl.BlockSpec(memory_space=pltpu.HBM)],
        out_specs=VM,
        scratch_shapes=[pltpu.SemaphoreType.DMA((2,))],
        compiler_params=pltpu.CompilerParams(vmem_limit_bytes=60 << 20),
        name="by_owner",
    )(grads)


def adamw_kernel(g_ref, w_ref, one_ref, two_ref, new_w_ref, new_one_ref, new_two_ref, copies_ref):
    gradient = g_ref[0].astype(jnp.float32)
    for j in range(1, 8):
        gradient = gradient + g_ref[j].astype(jnp.float32)
    master = w_ref[...]
    new_one = beta_one * one_ref[...] + (1.0 - beta_one) * gradient
    new_two = beta_two * two_ref[...] + (1.0 - beta_two) * gradient * gradient
    update = new_one / first_bias / (jnp.sqrt(new_two / second_bias) + epsilon)
    new_master = master - learning_rate * (update + weight_decay * master)
    new_one_ref[...] = new_one
    new_two_ref[...] = new_two
    new_w_ref[...] = new_master
    rollout = new_master.astype(jnp.bfloat16)
    for j in range(16):
        copies_ref[j] = rollout


def adamw(pieces, master, moment_one, moment_two):
    kept = jax.ShapeDtypeStruct(master.shape, jnp.float32)
    return pl.pallas_call(
        adamw_kernel,
        out_shape=(kept, kept, kept, jax.ShapeDtypeStruct((16,) + master.shape, jnp.bfloat16)),
        in_specs=[VM] * 4,
        out_specs=(VM,) * 4,
        compiler_params=PARAMS,
        name="adamw",
    )(pieces, master, moment_one, moment_two)


def split_kernel(me_ref, x_ref, *refs):
    blocks = refs[4]
    for b in range(4):
        v = [
            x_ref[:, :, 512 * b + 128 * k : 512 * b + 128 * (k + 1)].reshape(TOK, 128)
            for k in range(4)
        ]
        for half in range(2):
            cut = slice(64 * half, 64 * (half + 1))
            for p in range(2):
                blocks[2 * b + half, :, 128 * p : 128 * (p + 1)] = jnp.concatenate(
                    [v[2 * p][:, cut], v[2 * p + 1][:, cut]], axis=1
                )
    for p in range(4):
        for d in range(2):
            refs[p][d] = blocks[me_ref[0] ^ (2 * p + d)]


def split_features(me, x):
    pair = jax.ShapeDtypeStruct((2, TOK, COLS), jnp.bfloat16)
    return pl.pallas_call(
        split_kernel,
        out_shape=(pair,) * 4,
        in_specs=[SM, VM],
        out_specs=(VM,) * 4,
        scratch_shapes=[pltpu.VMEM((8, TOK, COLS), jnp.bfloat16)],
        compiler_params=PARAMS,
        name="split_features",
    )(me, x)


def project_kernel(me_ref, t_ref, xa, xb, xc, xd, w_ref, o_ref):
    me, own = me_ref[0], t_ref[0]
    for kv in range(2):
        w = jnp.concatenate(
            [w_ref[pl.ds(4 * (own ^ f), 4), kv].reshape(COLS, COLS) for f in range(4)], axis=0
        )
        for m in range(0, 8, 2):
            x = jnp.concatenate(
                [r[m : m + 2].reshape(2 * TOK, COLS) for r in (xa, xb, xc, xd)], axis=1
            )
            y = jnp.dot(x, w, preferred_element_type=jnp.float32).astype(jnp.bfloat16)
            for d in range(m, m + 2):
                o_ref[me ^ (2 * (d % 4) + d // 4), :, kv * COLS : (kv + 1) * COLS] = y[
                    TOK * (d - m) : TOK * (d - m + 1)
                ]


def project(me, own, features, w):
    return pl.pallas_call(
        project_kernel,
        out_shape=jax.ShapeDtypeStruct((8, TOK, 2 * COLS), jnp.bfloat16),
        in_specs=[SM] * 2 + [VM] * 5,
        out_specs=VM,
        compiler_params=PARAMS,
        name="project",
    )(me, own, *features, w)


def seen_bias(axis):
    width, old, count = PACK * (CACHE + STEPS), PACK * CACHE, 8 * PACK * STEPS
    shape = (count, width) if axis == 1 else (width, count)
    row = lax.broadcasted_iota(jnp.int32, shape, 1 - axis)
    col = lax.broadcasted_iota(jnp.int32, shape, axis)
    own = (row // STEPS) % PACK
    of_col = jnp.where(col < old, col // CACHE, (col - old) // STEPS)
    seen = (own == of_col) & ((col < old) | ((col - old) % STEPS <= row % STEPS))
    return jnp.where(seen, 0.0, -jnp.inf)


def length_bias(axis, lens):
    old = PACK * CACHE
    width = old + PACK * STEPS
    col = lax.broadcasted_iota(jnp.int32, (8, width) if axis == 1 else (width, 8 * PACK * STEPS), axis)
    limit = jnp.where(col < old, -1, width)
    for r in range(PACK):
        limit = jnp.where(col // CACHE == r, CACHE * r + lens[r], limit)
    return jnp.where(col < limit, 0.0, -jnp.inf)


def attend_kernel(lens_ref, part_ref, q_ref, k_ref, v_ref, o_ref):
    old, new = PACK * CACHE, PACK * STEPS
    width, count = old + new, 8 * new
    scale = 1.4426950408889634 / HD**0.5
    base, base_t = seen_bias(1), seen_bias(0)
    eye = lax.broadcasted_iota(jnp.int32, (count, count), 0) == lax.broadcasted_iota(
        jnp.int32, (count, count), 1
    )
    minus = jnp.full((width, count), -1.0, jnp.bfloat16)
    ones = jnp.ones((width, HD), jnp.bfloat16)
    heads = [[slice(HD * (8 * g + h), HD * (8 * g + h + 1)) for h in range(8)] for g in range(2)]
    across = (((1,), (1,)), ((), ()))
    for first in range(0, GROUPS, BATCH):
        units = []
        for i in range(first, first + BATCH):
            fresh = part_ref[0, new * i : new * (i + 1), :].astype(jnp.float32)
            for j in range(1, 8):
                fresh = fresh + part_ref[j, new * i : new * (i + 1), :].astype(jnp.float32)
            fresh = fresh.astype(jnp.bfloat16)
            rows = slice(PACK * i, PACK * (i + 1))
            past = slice(old * i, old * (i + 1))
            lens = [lens_ref[PACK * i + r] for r in range(PACK)]
            for g in range(2):
                k_lanes = slice(HD * g, HD * (g + 1))
                v_lanes = slice(COLS + HD * g, COLS + HD * (g + 1))
                q = jnp.concatenate([q_ref[rows, :, h].reshape(new, HD) for h in heads[g]], axis=0)
                k = jnp.concatenate([k_ref[past, k_lanes], fresh[:, k_lanes]], axis=0)
                v = jnp.concatenate([v_ref[past, k_lanes], fresh[:, v_lanes]], axis=0)
                units.append((rows, g, lens, q, k, v))
        turned = [
            lax.dot_general(k, q, across, preferred_element_type=jnp.float32)
            for rows, g, lens, q, k, v in units
        ]
        shifts = []
        for t, (rows, g, lens, q, k, v) in zip(turned, units):
            top = jnp.max(t + (base_t + length_bias(0, lens)), axis=0, keepdims=True)
            shifts.append(jnp.where(eye, top, 0.0).astype(jnp.bfloat16))
        scores = [
            lax.dot_general(
                jnp.concatenate([q, shift], axis=1),
                jnp.concatenate([k, minus], axis=1),
                across,
                preferred_element_type=jnp.float32,
            )
            for shift, (rows, g, lens, q, k, v) in zip(shifts, units)
        ]
        weights = [
            jnp.exp2(s * scale + (base + length_bias(1, lens)[0:1])).astype(jnp.bfloat16)
            for s, (rows, g, lens, q, k, v) in zip(scores, units)
        ]
        outs = [
            jnp.dot(e, jnp.concatenate([v, ones], axis=1), preferred_element_type=jnp.float32)
            for e, (rows, g, lens, q, k, v) in zip(weights, units)
        ]
        for out, (rows, g, lens, q, k, v) in zip(outs, units):
            out = (out[:, :HD] / out[:, HD:]).astype(jnp.bfloat16)
            for n, h in enumerate(heads[g]):
                o_ref[rows, :, h] = out[new * n : new * (n + 1)].reshape(PACK, STEPS, HD)


def attend(lengths, parts, q, keys, values):
    return pl.pallas_call(
        attend_kernel,
        out_shape=jax.ShapeDtypeStruct((ROWS, STEPS, FEAT), jnp.bfloat16),
        in_specs=[SM] + [VM] * 4,
        out_specs=VM,
        compiler_params=PARAMS,
        name="attend",
    )(lengths, parts, q, keys, values)


def flipped(x, axis):
    return lax.ppermute(x, axis, [(0, 1), (1, 0)])


def on_device(
    grad_parts, master_weight, moment_one, moment_two, layer_inputs, queries, kv_cache, lengths
):
    me = lax.axis_index(CUBE).astype(jnp.int32).reshape(1)
    own = lax.axis_index(TP).astype(jnp.int32).reshape(1)

    pieces = by_owner(grad_parts.reshape(1, 2, 8, 64, COLS))
    pieces = lax.all_to_all(pieces, FSDP, 0, 0, tiled=True)
    new_master, new_one, new_two, copies = adamw(pieces, master_weight, moment_one, moment_two)

    pairs = split_features(me, layer_inputs)
    pairs = [pairs[0]] + [
        lax.ppermute(pairs[p], ("yl", "xl"), [(i, i ^ p) for i in range(4)]) for p in range(1, 4)
    ]
    far = flipped(jnp.concatenate([pair[1:2] for pair in pairs]), "zl")
    features = jnp.concatenate([pair[0:1] for pair in pairs] + [far])
    beside = flipped(features, "c")
    across = flipped(features, "xh")
    beyond = flipped(across, "c")

    weight = lax.all_to_all(copies, FAR, 0, 0, tiled=True)

    partial = project(me, own, (features, beside, across, beyond), weight)
    partial = lax.all_to_all(partial, CUBE, 0, 0, tiled=True)

    keys = kv_cache[:, :, 0].reshape(ROWS * CACHE, COLS)
    values = kv_cache[:, :, 1].reshape(ROWS * CACHE, COLS)
    context = attend(lengths, partial, queries, keys, values)
    return (new_master, new_one, new_two, context)


def solution(mesh):
    finer = Mesh(mesh.devices.reshape(4, 2, 2, 4, 2, 2, 2), AXES)
    shard = P(None, SHARD, TP)
    return jax.shard_map(
        on_device,
        mesh=finer,
        in_specs=(
            P(FSDP, None, REP, TP),
            shard,
            shard,
            shard,
            P(SHARD, None, TP),
            P(SHARD, None, TP),
            P(SHARD, None, None, TP),
            P(SHARD),
        ),
        out_specs=(shard, shard, shard, P(SHARD, None, TP)),
        check_vma=False,
    )
```

```python
import jax
import jax.numpy as jnp
from jax import lax
from jax.experimental import pallas as pl
from jax.experimental.pallas import tpu as pltpu
from jax.sharding import Mesh
from jax.sharding import PartitionSpec as P

HD = 128
ROWS = 48
STEPS = 4
TOK = ROWS * STEPS
CACHE = 24
FEAT = 2048
COLS = 256
PACK = 4
GROUPS = ROWS // PACK
BATCH = 4
AXES = ("yh", "yl", "xl", "zh", "zl", "xh", "c")
SHARD = ("yh", "yl", "xl", "zh", "zl")
REP = ("yh", "yl", "xl")
FSDP = ("zh", "zl")
TP = ("xh", "c")
CUBE = ("yl", "xl", "zl")
FAR = ("yh", "zh")

beta_one = 0.9
beta_two = 0.95
learning_rate = 0.001
weight_decay = 0.1
epsilon = 1e-08
first_bias = 1.0 - 0.9**10
second_bias = 1.0 - 0.95**10


VM = pl.BlockSpec(memory_space=pltpu.VMEM)
SM = pl.BlockSpec(memory_space=pltpu.SMEM)
PARAMS = pltpu.CompilerParams(vmem_limit_bytes=40 << 20)


def by_owner_kernel(g_ref, o_ref, sems):
    copies = [
        pltpu.make_async_copy(g_ref.at[0, kv], o_ref.at[:, kv], sems.at[kv]) for kv in range(2)
    ]
    for copy in copies:
        copy.start()
    for copy in copies:
        copy.wait()


def by_owner(grads):
    return pl.pallas_call(
        by_owner_kernel,
        out_shape=jax.ShapeDtypeStruct((8, 2, 64, COLS), jnp.bfloat16),
        in_specs=[pl.BlockSpec(memory_space=pltpu.HBM)],
        out_specs=VM,
        scratch_shapes=[pltpu.SemaphoreType.DMA((2,))],
        compiler_params=pltpu.CompilerParams(vmem_limit_bytes=60 << 20),
        name="by_owner",
    )(grads)


def adamw_kernel(g_ref, w_ref, one_ref, two_ref, new_w_ref, new_one_ref, new_two_ref, copies_ref):
    gradient = g_ref[0].astype(jnp.float32)
    for j in range(1, 8):
        gradient = gradient + g_ref[j].astype(jnp.float32)
    master = w_ref[...]
    new_one = beta_one * one_ref[...] + (1.0 - beta_one) * gradient
    new_two = beta_two * two_ref[...] + (1.0 - beta_two) * gradient * gradient
    update = new_one / first_bias / (jnp.sqrt(new_two / second_bias) + epsilon)
    new_master = master - learning_rate * (update + weight_decay * master)
    new_one_ref[...] = new_one
    new_two_ref[...] = new_two
    new_w_ref[...] = new_master
    rollout = new_master.astype(jnp.bfloat16)
    for j in range(16):
        copies_ref[j] = rollout


def adamw(pieces, master, moment_one, moment_two):
    kept = jax.ShapeDtypeStruct(master.shape, jnp.float32)
    return pl.pallas_call(
        adamw_kernel,
        out_shape=(kept, kept, kept, jax.ShapeDtypeStruct((16,) + master.shape, jnp.bfloat16)),
        in_specs=[VM] * 4,
        out_specs=(VM,) * 4,
        compiler_params=PARAMS,
        name="adamw",
    )(pieces, master, moment_one, moment_two)


def split_kernel(me_ref, x_ref, *refs):
    blocks = refs[4]
    for b in range(4):
        v = [
            x_ref[:, :, 512 * b + 128 * k : 512 * b + 128 * (k + 1)].reshape(TOK, 128)
            for k in range(4)
        ]
        for half in range(2):
            cut = slice(64 * half, 64 * (half + 1))
            for p in range(2):
                blocks[2 * b + half, :, 128 * p : 128 * (p + 1)] = jnp.concatenate(
                    [v[2 * p][:, cut], v[2 * p + 1][:, cut]], axis=1
                )
    for p in range(4):
        for d in range(2):
            refs[p][d] = blocks[me_ref[0] ^ (2 * p + d)]


def split_features(me, x):
    pair = jax.ShapeDtypeStruct((2, TOK, COLS), jnp.bfloat16)
    return pl.pallas_call(
        split_kernel,
        out_shape=(pair,) * 4,
        in_specs=[SM, VM],
        out_specs=(VM,) * 4,
        scratch_shapes=[pltpu.VMEM((8, TOK, COLS), jnp.bfloat16)],
        compiler_params=PARAMS,
        name="split_features",
    )(me, x)


def project_kernel(me_ref, t_ref, xa, xb, xc, xd, w_ref, o_ref):
    me, own = me_ref[0], t_ref[0]
    for kv in range(2):
        w = jnp.concatenate(
            [w_ref[pl.ds(4 * (own ^ f), 4), kv].reshape(COLS, COLS) for f in range(4)], axis=0
        )
        for m in range(0, 8, 2):
            x = jnp.concatenate(
                [r[m : m + 2].reshape(2 * TOK, COLS) for r in (xa, xb, xc, xd)], axis=1
            )
            y = jnp.dot(x, w, preferred_element_type=jnp.float32)
            for d in range(m, m + 2):
                o_ref[me ^ (2 * (d % 4) + d // 4), :, kv * COLS : (kv + 1) * COLS] = y[
                    TOK * (d - m) : TOK * (d - m + 1)
                ]


def project(me, own, features, w):
    return pl.pallas_call(
        project_kernel,
        out_shape=jax.ShapeDtypeStruct((8, TOK, 2 * COLS), jnp.float32),
        in_specs=[SM] * 2 + [VM] * 5,
        out_specs=VM,
        compiler_params=PARAMS,
        name="project",
    )(me, own, *features, w)


def seen_bias(axis):
    width, old, count = PACK * (CACHE + STEPS), PACK * CACHE, 8 * PACK * STEPS
    shape = (count, width) if axis == 1 else (width, count)
    row = lax.broadcasted_iota(jnp.int32, shape, 1 - axis)
    col = lax.broadcasted_iota(jnp.int32, shape, axis)
    own = (row // STEPS) % PACK
    of_col = jnp.where(col < old, col // CACHE, (col - old) // STEPS)
    seen = (own == of_col) & ((col < old) | ((col - old) % STEPS <= row % STEPS))
    return jnp.where(seen, 0.0, -jnp.inf)


def length_bias(axis, lens):
    old = PACK * CACHE
    width = old + PACK * STEPS
    col = lax.broadcasted_iota(jnp.int32, (8, width) if axis == 1 else (width, 8 * PACK * STEPS), axis)
    limit = jnp.where(col < old, -1, width)
    for r in range(PACK):
        limit = jnp.where(col // CACHE == r, CACHE * r + lens[r], limit)
    return jnp.where(col < limit, 0.0, -jnp.inf)


def attend_kernel(lens_ref, fresh_ref, q_ref, k_ref, v_ref, o_ref):
    old, new = PACK * CACHE, PACK * STEPS
    width, count = old + new, 8 * new
    scale = 1.4426950408889634 / HD**0.5
    base, base_t = seen_bias(1), seen_bias(0)
    eye = lax.broadcasted_iota(jnp.int32, (count, count), 0) == lax.broadcasted_iota(
        jnp.int32, (count, count), 1
    )
    minus = jnp.full((width, count), -1.0, jnp.bfloat16)
    ones = jnp.ones((width, HD), jnp.bfloat16)
    heads = [[slice(HD * (8 * g + h), HD * (8 * g + h + 1)) for h in range(8)] for g in range(2)]
    across = (((1,), (1,)), ((), ()))
    for first in range(0, GROUPS, BATCH):
        units = []
        for i in range(first, first + BATCH):
            fresh = fresh_ref[new * i : new * (i + 1), :]
            rows = slice(PACK * i, PACK * (i + 1))
            past = slice(old * i, old * (i + 1))
            lens = [lens_ref[PACK * i + r] for r in range(PACK)]
            for g in range(2):
                k_lanes = slice(HD * g, HD * (g + 1))
                v_lanes = slice(COLS + HD * g, COLS + HD * (g + 1))
                q = jnp.concatenate([q_ref[rows, :, h].reshape(new, HD) for h in heads[g]], axis=0)
                k = jnp.concatenate([k_ref[past, k_lanes], fresh[:, k_lanes]], axis=0)
                v = jnp.concatenate([v_ref[past, k_lanes], fresh[:, v_lanes]], axis=0)
                units.append((rows, g, lens, q, k, v))
        turned = [
            lax.dot_general(k, q, across, preferred_element_type=jnp.float32)
            for rows, g, lens, q, k, v in units
        ]
        shifts = []
        for t, (rows, g, lens, q, k, v) in zip(turned, units):
            top = jnp.max(t + (base_t + length_bias(0, lens)), axis=0, keepdims=True)
            shifts.append(jnp.where(eye, top, 0.0).astype(jnp.bfloat16))
        scores = [
            lax.dot_general(
                jnp.concatenate([q, shift], axis=1),
                jnp.concatenate([k, minus], axis=1),
                across,
                preferred_element_type=jnp.float32,
            )
            for shift, (rows, g, lens, q, k, v) in zip(shifts, units)
        ]
        weights = [
            jnp.exp2(s * scale + (base + length_bias(1, lens)[0:1])).astype(jnp.bfloat16)
            for s, (rows, g, lens, q, k, v) in zip(scores, units)
        ]
        outs = [
            jnp.dot(e, jnp.concatenate([v, ones], axis=1), preferred_element_type=jnp.float32)
            for e, (rows, g, lens, q, k, v) in zip(weights, units)
        ]
        for out, (rows, g, lens, q, k, v) in zip(outs, units):
            out = (out[:, :HD] / out[:, HD:]).astype(jnp.bfloat16)
            for n, h in enumerate(heads[g]):
                o_ref[rows, :, h] = out[new * n : new * (n + 1)].reshape(PACK, STEPS, HD)


def attend(lengths, fresh, q, keys, values):
    return pl.pallas_call(
        attend_kernel,
        out_shape=jax.ShapeDtypeStruct((ROWS, STEPS, FEAT), jnp.bfloat16),
        in_specs=[SM] + [VM] * 4,
        out_specs=VM,
        compiler_params=PARAMS,
        name="attend",
    )(lengths, fresh, q, keys, values)


def flipped(x, axis):
    return lax.ppermute(x, axis, [(0, 1), (1, 0)])


def on_device(
    grad_parts, master_weight, moment_one, moment_two, layer_inputs, queries, kv_cache, lengths
):
    me = lax.axis_index(CUBE).astype(jnp.int32).reshape(1)
    own = lax.axis_index(TP).astype(jnp.int32).reshape(1)

    pieces = by_owner(grad_parts.reshape(1, 2, 8, 64, COLS))
    pieces = lax.all_to_all(pieces, FSDP, 0, 0, tiled=True)
    new_master, new_one, new_two, copies = adamw(pieces, master_weight, moment_one, moment_two)

    pairs = split_features(me, layer_inputs)
    pairs = [pairs[0]] + [
        lax.ppermute(pairs[p], ("yl", "xl"), [(i, i ^ p) for i in range(4)]) for p in range(1, 4)
    ]
    far = flipped(jnp.concatenate([pair[1:2] for pair in pairs]), "zl")
    features = jnp.concatenate([pair[0:1] for pair in pairs] + [far])
    beside = flipped(features, "c")
    across = flipped(features, "xh")
    beyond = flipped(across, "c")

    weight = lax.all_to_all(copies, FAR, 0, 0, tiled=True)

    partial = project(me, own, (features, beside, across, beyond), weight)
    partial = (partial * 64.0).astype(jnp.float16)
    partial = lax.all_to_all(partial, CUBE, 0, 0, tiled=True)
    fresh = (jnp.sum(partial.astype(jnp.float32), axis=0) * (1.0 / 64.0)).astype(jnp.bfloat16)

    keys = kv_cache[:, :, 0].reshape(ROWS * CACHE, COLS)
    values = kv_cache[:, :, 1].reshape(ROWS * CACHE, COLS)
    context = attend(lengths, fresh, queries, keys, values)
    return (new_master, new_one, new_two, context)


def solution(mesh):
    finer = Mesh(mesh.devices.reshape(4, 2, 2, 4, 2, 2, 2), AXES)
    shard = P(None, SHARD, TP)
    return jax.shard_map(
        on_device,
        mesh=finer,
        in_specs=(
            P(FSDP, None, REP, TP),
            shard,
            shard,
            shard,
            P(SHARD, None, TP),
            P(SHARD, None, TP),
            P(SHARD, None, None, TP),
            P(SHARD),
        ),
        out_specs=(shard, shard, shard, P(SHARD, None, TP)),
        check_vma=False,
    )
```

```python
import jax
import jax.numpy as jnp
from jax import lax
from jax.experimental import pallas as pl
from jax.experimental.pallas import tpu as pltpu
from jax.sharding import Mesh
from jax.sharding import PartitionSpec as P

HD = 128
ROWS = 48
STEPS = 4
TOK = ROWS * STEPS
CACHE = 24
FEAT = 2048
COLS = 256
PACK = 4
GROUPS = ROWS // PACK
BATCH = 4
AXES = ("yh", "yl", "xl", "zh", "zl", "xh", "c")
SHARD = ("yh", "yl", "xl", "zh", "zl")
REP = ("yh", "yl", "xl")
FSDP = ("zh", "zl")
TP = ("xh", "c")
CUBE = ("yl", "xl", "zl")
FAR = ("yh", "zh")

beta_one = 0.9
beta_two = 0.95
learning_rate = 0.001
weight_decay = 0.1
epsilon = 1e-08
first_bias = 1.0 - 0.9**10
second_bias = 1.0 - 0.95**10


VM = pl.BlockSpec(memory_space=pltpu.VMEM)
SM = pl.BlockSpec(memory_space=pltpu.SMEM)
PARAMS = pltpu.CompilerParams(vmem_limit_bytes=40 << 20)


def by_owner_kernel(g_ref, o_ref, sems):
    copies = [
        pltpu.make_async_copy(g_ref.at[0, kv], o_ref.at[:, kv], sems.at[kv]) for kv in range(2)
    ]
    for copy in copies:
        copy.start()
    for copy in copies:
        copy.wait()


def by_owner(grads):
    return pl.pallas_call(
        by_owner_kernel,
        out_shape=jax.ShapeDtypeStruct((8, 2, 64, COLS), jnp.bfloat16),
        in_specs=[pl.BlockSpec(memory_space=pltpu.HBM)],
        out_specs=VM,
        scratch_shapes=[pltpu.SemaphoreType.DMA((2,))],
        compiler_params=pltpu.CompilerParams(vmem_limit_bytes=60 << 20),
        name="by_owner",
    )(grads)


def adamw_kernel(g_ref, w_ref, one_ref, two_ref, new_w_ref, new_one_ref, new_two_ref, copies_ref):
    gradient = g_ref[0].astype(jnp.float32)
    for j in range(1, 8):
        gradient = gradient + g_ref[j].astype(jnp.float32)
    master = w_ref[...]
    new_one = beta_one * one_ref[...] + (1.0 - beta_one) * gradient
    new_two = beta_two * two_ref[...] + (1.0 - beta_two) * gradient * gradient
    update = new_one / first_bias / (jnp.sqrt(new_two / second_bias) + epsilon)
    new_master = master - learning_rate * (update + weight_decay * master)
    new_one_ref[...] = new_one
    new_two_ref[...] = new_two
    new_w_ref[...] = new_master
    rollout = new_master.astype(jnp.bfloat16)
    for j in range(16):
        copies_ref[j] = rollout


def adamw(pieces, master, moment_one, moment_two):
    kept = jax.ShapeDtypeStruct(master.shape, jnp.float32)
    return pl.pallas_call(
        adamw_kernel,
        out_shape=(kept, kept, kept, jax.ShapeDtypeStruct((16,) + master.shape, jnp.bfloat16)),
        in_specs=[VM] * 4,
        out_specs=(VM,) * 4,
        compiler_params=PARAMS,
        name="adamw",
    )(pieces, master, moment_one, moment_two)


def split_kernel(me_ref, x_ref, kept_ref, sent_ref, blocks):
    for b in range(4):
        v = [
            x_ref[:, :, 512 * b + 128 * k : 512 * b + 128 * (k + 1)].reshape(TOK, 128)
            for k in range(4)
        ]
        for half in range(2):
            cut = slice(64 * half, 64 * (half + 1))
            for p in range(2):
                blocks[2 * b + half, :, 128 * p : 128 * (p + 1)] = jnp.concatenate(
                    [v[2 * p][:, cut], v[2 * p + 1][:, cut]], axis=1
                )
    for d in range(4):
        away = d // 2 + 2 * (d % 2)
        kept_ref[d] = blocks[me_ref[0] ^ away]
        sent_ref[d] = blocks[me_ref[0] ^ away ^ 4]


def split_features(me, x):
    half = jax.ShapeDtypeStruct((4, TOK, COLS), jnp.bfloat16)
    return pl.pallas_call(
        split_kernel,
        out_shape=(half, half),
        in_specs=[SM, VM],
        out_specs=(VM, VM),
        scratch_shapes=[pltpu.VMEM((8, TOK, COLS), jnp.bfloat16)],
        compiler_params=PARAMS,
        name="split_features",
    )(me, x)


def project_kernel(me_ref, t_ref, *refs):
    w_ref, o_ref = refs[8], refs[9]
    me, own = me_ref[0], t_ref[0]
    for kv in range(2):
        w = jnp.concatenate(
            [w_ref[pl.ds(4 * (own ^ f), 4), kv].reshape(COLS, COLS) for f in range(4)], axis=0
        )
        for half in range(2):
            for m in range(0, 4, 2):
                x = jnp.concatenate(
                    [refs[2 * f + half][m : m + 2].reshape(2 * TOK, COLS) for f in range(4)],
                    axis=1,
                )
                y = jnp.dot(x, w, preferred_element_type=jnp.float32)
                for d in range(2):
                    o_ref[me ^ (m // 2 + 4 * d + 2 * half), :, kv * COLS : (kv + 1) * COLS] = y[
                        TOK * d : TOK * (d + 1)
                    ]


def project(me, own, features, w):
    return pl.pallas_call(
        project_kernel,
        out_shape=jax.ShapeDtypeStruct((8, TOK, 2 * COLS), jnp.float32),
        in_specs=[SM] * 2 + [VM] * 9,
        out_specs=VM,
        compiler_params=PARAMS,
        name="project",
    )(me, own, *features, w)


def seen_bias(axis):
    width, old, count = PACK * (CACHE + STEPS), PACK * CACHE, 8 * PACK * STEPS
    shape = (count, width) if axis == 1 else (width, count)
    row = lax.broadcasted_iota(jnp.int32, shape, 1 - axis)
    col = lax.broadcasted_iota(jnp.int32, shape, axis)
    own = (row // STEPS) % PACK
    of_col = jnp.where(col < old, col // CACHE, (col - old) // STEPS)
    seen = (own == of_col) & ((col < old) | ((col - old) % STEPS <= row % STEPS))
    return jnp.where(seen, 0.0, -jnp.inf)


def length_bias(axis, lens):
    old = PACK * CACHE
    width = old + PACK * STEPS
    col = lax.broadcasted_iota(jnp.int32, (8, width) if axis == 1 else (width, 8 * PACK * STEPS), axis)
    limit = jnp.where(col < old, -1, width)
    for r in range(PACK):
        limit = jnp.where(col // CACHE == r, CACHE * r + lens[r], limit)
    return jnp.where(col < limit, 0.0, -jnp.inf)


def attend_kernel(lens_ref, fresh_ref, q_ref, k_ref, v_ref, o_ref):
    old, new = PACK * CACHE, PACK * STEPS
    width, count = old + new, 8 * new
    scale = 1.4426950408889634 / HD**0.5
    base, base_t = seen_bias(1), seen_bias(0)
    eye = lax.broadcasted_iota(jnp.int32, (count, count), 0) == lax.broadcasted_iota(
        jnp.int32, (count, count), 1
    )
    minus = jnp.full((width, count), -1.0, jnp.bfloat16)
    ones = jnp.ones((width, HD), jnp.bfloat16)
    heads = [[slice(HD * (8 * g + h), HD * (8 * g + h + 1)) for h in range(8)] for g in range(2)]
    across = (((1,), (1,)), ((), ()))
    for first in range(0, GROUPS, BATCH):
        units = []
        for i in range(first, first + BATCH):
            fresh = fresh_ref[new * i : new * (i + 1), :]
            rows = slice(PACK * i, PACK * (i + 1))
            past = slice(old * i, old * (i + 1))
            lens = [lens_ref[PACK * i + r] for r in range(PACK)]
            for g in range(2):
                k_lanes = slice(HD * g, HD * (g + 1))
                v_lanes = slice(COLS + HD * g, COLS + HD * (g + 1))
                q = jnp.concatenate([q_ref[rows, :, h].reshape(new, HD) for h in heads[g]], axis=0)
                k = jnp.concatenate([k_ref[past, k_lanes], fresh[:, k_lanes]], axis=0)
                v = jnp.concatenate([v_ref[past, k_lanes], fresh[:, v_lanes]], axis=0)
                units.append((rows, g, lens, q, k, v))
        turned = [
            lax.dot_general(k, q, across, preferred_element_type=jnp.float32)
            for rows, g, lens, q, k, v in units
        ]
        shifts = []
        for t, (rows, g, lens, q, k, v) in zip(turned, units):
            top = jnp.max(t + (base_t + length_bias(0, lens)), axis=0, keepdims=True)
            shifts.append(jnp.where(eye, top, 0.0).astype(jnp.bfloat16))
        scores = [
            lax.dot_general(
                jnp.concatenate([q, shift], axis=1),
                jnp.concatenate([k, minus], axis=1),
                across,
                preferred_element_type=jnp.float32,
            )
            for shift, (rows, g, lens, q, k, v) in zip(shifts, units)
        ]
        weights = [
            jnp.exp2(s * scale + (base + length_bias(1, lens)[0:1])).astype(jnp.bfloat16)
            for s, (rows, g, lens, q, k, v) in zip(scores, units)
        ]
        outs = [
            jnp.dot(e, jnp.concatenate([v, ones], axis=1), preferred_element_type=jnp.float32)
            for e, (rows, g, lens, q, k, v) in zip(weights, units)
        ]
        for out, (rows, g, lens, q, k, v) in zip(outs, units):
            out = (out[:, :HD] / out[:, HD:]).astype(jnp.bfloat16)
            for n, h in enumerate(heads[g]):
                o_ref[rows, :, h] = out[new * n : new * (n + 1)].reshape(PACK, STEPS, HD)


def attend(lengths, fresh, q, keys, values):
    return pl.pallas_call(
        attend_kernel,
        out_shape=jax.ShapeDtypeStruct((ROWS, STEPS, FEAT), jnp.bfloat16),
        in_specs=[SM] + [VM] * 4,
        out_specs=VM,
        compiler_params=PARAMS,
        name="attend",
    )(lengths, fresh, q, keys, values)


def flipped(x, axis):
    return lax.ppermute(x, axis, [(0, 1), (1, 0)])


def on_device(
    grad_parts, master_weight, moment_one, moment_two, layer_inputs, queries, kv_cache, lengths
):
    me = lax.axis_index(CUBE).astype(jnp.int32).reshape(1)
    own = lax.axis_index(TP).astype(jnp.int32).reshape(1)

    pieces = by_owner(grad_parts.reshape(1, 2, 8, 64, COLS))
    pieces = lax.all_to_all(pieces, FSDP, 0, 0, tiled=True)
    new_master, new_one, new_two, copies = adamw(pieces, master_weight, moment_one, moment_two)

    kept, sent = split_features(me, layer_inputs)
    by_y = flipped(sent, "yl")
    by_z = flipped(jnp.concatenate([kept[2:4], by_y[2:4]]), "zl")
    near = jnp.concatenate([kept[0:1], by_y[0:1], by_z[0:1], by_z[2:3]])
    far = flipped(jnp.concatenate([kept[1:2], by_y[1:2], by_z[1:2], by_z[3:4]]), "xl")
    features = []
    for half in (near, far):
        across = flipped(half, "xh")
        features.append((half, flipped(half, "c"), across, flipped(across, "c")))
    features = [features[h][f] for f in range(4) for h in range(2)]

    weight = lax.all_to_all(copies, FAR, 0, 0, tiled=True)

    partial = project(me, own, features, weight)
    partial = (partial * 64.0).astype(jnp.float16)
    partial = lax.all_to_all(partial, CUBE, 0, 0, tiled=True)
    fresh = (jnp.sum(partial.astype(jnp.float32), axis=0) * (1.0 / 64.0)).astype(jnp.bfloat16)

    keys = kv_cache[:, :, 0].reshape(ROWS * CACHE, COLS)
    values = kv_cache[:, :, 1].reshape(ROWS * CACHE, COLS)
    context = attend(lengths, fresh, queries, keys, values)
    return (new_master, new_one, new_two, context)


def solution(mesh):
    finer = Mesh(mesh.devices.reshape(4, 2, 2, 4, 2, 2, 2), AXES)
    shard = P(None, SHARD, TP)
    return jax.shard_map(
        on_device,
        mesh=finer,
        in_specs=(
            P(FSDP, None, REP, TP),
            shard,
            shard,
            shard,
            P(SHARD, None, TP),
            P(SHARD, None, TP),
            P(SHARD, None, None, TP),
            P(SHARD),
        ),
        out_specs=(shard, shard, shard, P(SHARD, None, TP)),
        check_vma=False,
    )
```

```python
import jax
import jax.numpy as jnp
from jax import lax
from jax.experimental import pallas as pl
from jax.experimental.pallas import tpu as pltpu
from jax.sharding import Mesh
from jax.sharding import PartitionSpec as P

HD = 128
ROWS = 48
STEPS = 4
TOK = ROWS * STEPS
CACHE = 24
FEAT = 2048
COLS = 256
PACK = 4
GROUPS = ROWS // PACK
BATCH = 4
AXES = ("yh", "yl", "xl", "zh", "zl", "xh", "c")
SHARD = ("yh", "yl", "xl", "zh", "zl")
REP = ("yh", "yl", "xl")
FSDP = ("zh", "zl")
TP = ("xh", "c")
CUBE = ("yl", "xl", "zl")
FAR = ("yh", "zh")

beta_one = 0.9
beta_two = 0.95
learning_rate = 0.001
weight_decay = 0.1
epsilon = 1e-08
first_bias = 1.0 - 0.9**10
second_bias = 1.0 - 0.95**10


VM = pl.BlockSpec(memory_space=pltpu.VMEM)
SM = pl.BlockSpec(memory_space=pltpu.SMEM)
PARAMS = pltpu.CompilerParams(vmem_limit_bytes=40 << 20)


def by_owner_kernel(g_ref, o_ref, sems):
    copies = [
        pltpu.make_async_copy(g_ref.at[0, kv], o_ref.at[:, kv], sems.at[kv]) for kv in range(2)
    ]
    for copy in copies:
        copy.start()
    for copy in copies:
        copy.wait()


def by_owner(grads):
    return pl.pallas_call(
        by_owner_kernel,
        out_shape=jax.ShapeDtypeStruct((8, 2, 64, COLS), jnp.bfloat16),
        in_specs=[pl.BlockSpec(memory_space=pltpu.HBM)],
        out_specs=VM,
        scratch_shapes=[pltpu.SemaphoreType.DMA((2,))],
        compiler_params=pltpu.CompilerParams(vmem_limit_bytes=60 << 20),
        name="by_owner",
    )(grads)


def adamw_kernel(g_ref, w_ref, one_ref, two_ref, new_w_ref, new_one_ref, new_two_ref, copies_ref):
    gradient = g_ref[0].astype(jnp.float32)
    for j in range(1, 8):
        gradient = gradient + g_ref[j].astype(jnp.float32)
    master = w_ref[...]
    new_one = beta_one * one_ref[...] + (1.0 - beta_one) * gradient
    new_two = beta_two * two_ref[...] + (1.0 - beta_two) * gradient * gradient
    update = new_one / first_bias / (jnp.sqrt(new_two / second_bias) + epsilon)
    new_master = master - learning_rate * (update + weight_decay * master)
    new_one_ref[...] = new_one
    new_two_ref[...] = new_two
    new_w_ref[...] = new_master
    rollout = new_master.astype(jnp.bfloat16)
    for j in range(16):
        copies_ref[j] = rollout


def adamw(pieces, master, moment_one, moment_two):
    kept = jax.ShapeDtypeStruct(master.shape, jnp.float32)
    return pl.pallas_call(
        adamw_kernel,
        out_shape=(kept, kept, kept, jax.ShapeDtypeStruct((16,) + master.shape, jnp.bfloat16)),
        in_specs=[VM] * 4,
        out_specs=(VM,) * 4,
        compiler_params=PARAMS,
        name="adamw",
    )(pieces, master, moment_one, moment_two)


def split_kernel(me_ref, x_ref, kept_ref, sent_ref, blocks):
    for b in range(4):
        v = [
            x_ref[:, :, 512 * b + 128 * k : 512 * b + 128 * (k + 1)].reshape(TOK, 128)
            for k in range(4)
        ]
        for half in range(2):
            cut = slice(64 * half, 64 * (half + 1))
            for p in range(2):
                blocks[2 * b + half, :, 128 * p : 128 * (p + 1)] = jnp.concatenate(
                    [v[2 * p][:, cut], v[2 * p + 1][:, cut]], axis=1
                )
    for d in range(4):
        away = d // 2 + 2 * (d % 2)
        kept_ref[d] = blocks[me_ref[0] ^ away]
        sent_ref[d] = blocks[me_ref[0] ^ away ^ 4]


def split_features(me, x):
    half = jax.ShapeDtypeStruct((4, TOK, COLS), jnp.bfloat16)
    return pl.pallas_call(
        split_kernel,
        out_shape=(half, half),
        in_specs=[SM, VM],
        out_specs=(VM, VM),
        scratch_shapes=[pltpu.VMEM((8, TOK, COLS), jnp.bfloat16)],
        compiler_params=PARAMS,
        name="split_features",
    )(me, x)


def project_kernel(me_ref, t_ref, *refs):
    w_ref, o_ref = refs[8], refs[9]
    me, own = me_ref[0], t_ref[0]
    for kv in range(2):
        w = jnp.concatenate(
            [w_ref[pl.ds(4 * (own ^ f), 4), kv].reshape(COLS, COLS) for f in range(4)], axis=0
        )
        for half in range(2):
            for m in range(0, 4, 2):
                x = jnp.concatenate(
                    [refs[2 * f + half][m : m + 2].reshape(2 * TOK, COLS) for f in range(4)],
                    axis=1,
                )
                y = jnp.dot(x, w, preferred_element_type=jnp.float32)
                for d in range(2):
                    o_ref[me ^ (m // 2 + 4 * d + 2 * half), :, kv * COLS : (kv + 1) * COLS] = y[
                        TOK * d : TOK * (d + 1)
                    ]


def project(me, own, features, w):
    return pl.pallas_call(
        project_kernel,
        out_shape=jax.ShapeDtypeStruct((8, TOK, 2 * COLS), jnp.float32),
        in_specs=[SM] * 2 + [VM] * 9,
        out_specs=VM,
        compiler_params=PARAMS,
        name="project",
    )(me, own, *features, w)


def seen_bias(axis):
    width, old, count = PACK * (CACHE + STEPS), PACK * CACHE, 8 * PACK * STEPS
    shape = (count, width) if axis == 1 else (width, count)
    row = lax.broadcasted_iota(jnp.int32, shape, 1 - axis)
    col = lax.broadcasted_iota(jnp.int32, shape, axis)
    own = (row // STEPS) % PACK
    of_col = jnp.where(col < old, col // CACHE, (col - old) // STEPS)
    seen = (own == of_col) & ((col < old) | ((col - old) % STEPS <= row % STEPS))
    return jnp.where(seen, 0.0, -jnp.inf)


def length_bias(axis, lens):
    old = PACK * CACHE
    width = old + PACK * STEPS
    col = lax.broadcasted_iota(jnp.int32, (8, width) if axis == 1 else (width, 8 * PACK * STEPS), axis)
    limit = jnp.where(col < old, -1, width)
    for r in range(PACK):
        limit = jnp.where(col // CACHE == r, CACHE * r + lens[r], limit)
    return jnp.where(col < limit, 0.0, -jnp.inf)


def attend_kernel(lens_ref, fresh_ref, q_ref, k_ref, v_ref, o_ref):
    old, new = PACK * CACHE, PACK * STEPS
    width, count = old + new, 8 * new
    scale = 1.4426950408889634 / HD**0.5
    base, base_t = seen_bias(1), seen_bias(0)
    eye = lax.broadcasted_iota(jnp.int32, (count, count), 0) == lax.broadcasted_iota(
        jnp.int32, (count, count), 1
    )
    minus = jnp.full((width, count), -1.0, jnp.bfloat16)
    ones = jnp.ones((width, HD), jnp.bfloat16)
    heads = [[slice(HD * (8 * g + h), HD * (8 * g + h + 1)) for h in range(8)] for g in range(2)]
    across = (((1,), (1,)), ((), ()))
    for first in range(0, GROUPS, BATCH):
        units = []
        for i in range(first, first + BATCH):
            fresh = fresh_ref[new * i : new * (i + 1), :]
            rows = slice(PACK * i, PACK * (i + 1))
            past = slice(old * i, old * (i + 1))
            lens = [lens_ref[PACK * i + r] for r in range(PACK)]
            for g in range(2):
                k_lanes = slice(HD * g, HD * (g + 1))
                v_lanes = slice(COLS + HD * g, COLS + HD * (g + 1))
                q = jnp.concatenate([q_ref[rows, :, h].reshape(new, HD) for h in heads[g]], axis=0)
                k = jnp.concatenate([k_ref[past, k_lanes], fresh[:, k_lanes]], axis=0)
                v = jnp.concatenate([v_ref[past, k_lanes], fresh[:, v_lanes]], axis=0)
                units.append((rows, g, lens, q, k, v))
        turned = [
            lax.dot_general(k, q, across, preferred_element_type=jnp.float32)
            for rows, g, lens, q, k, v in units
        ]
        shifts = []
        for t, (rows, g, lens, q, k, v) in zip(turned, units):
            top = jnp.max(t + (base_t + length_bias(0, lens)), axis=0, keepdims=True)
            high = top.astype(jnp.bfloat16).astype(jnp.float32)
            shifts.append(
                [jnp.where(eye, part, 0.0).astype(jnp.bfloat16) for part in (high, top - high)]
            )
        scores = [
            lax.dot_general(
                jnp.concatenate([q] + shift, axis=1),
                jnp.concatenate([k, minus, minus], axis=1),
                across,
                preferred_element_type=jnp.float32,
            )
            for shift, (rows, g, lens, q, k, v) in zip(shifts, units)
        ]
        weights = [
            jnp.exp2(s * scale + (base + length_bias(1, lens)[0:1])).astype(jnp.bfloat16)
            for s, (rows, g, lens, q, k, v) in zip(scores, units)
        ]
        outs = [
            jnp.dot(e, jnp.concatenate([v, ones], axis=1), preferred_element_type=jnp.float32)
            for e, (rows, g, lens, q, k, v) in zip(weights, units)
        ]
        for out, (rows, g, lens, q, k, v) in zip(outs, units):
            out = (out[:, :HD] / out[:, HD:]).astype(jnp.bfloat16)
            for n, h in enumerate(heads[g]):
                o_ref[rows, :, h] = out[new * n : new * (n + 1)].reshape(PACK, STEPS, HD)


def attend(lengths, fresh, q, keys, values):
    return pl.pallas_call(
        attend_kernel,
        out_shape=jax.ShapeDtypeStruct((ROWS, STEPS, FEAT), jnp.bfloat16),
        in_specs=[SM] + [VM] * 4,
        out_specs=VM,
        compiler_params=PARAMS,
        name="attend",
    )(lengths, fresh, q, keys, values)


def flipped(x, axis):
    return lax.ppermute(x, axis, [(0, 1), (1, 0)])


def on_device(
    grad_parts, master_weight, moment_one, moment_two, layer_inputs, queries, kv_cache, lengths
):
    me = lax.axis_index(CUBE).astype(jnp.int32).reshape(1)
    own = lax.axis_index(TP).astype(jnp.int32).reshape(1)

    pieces = by_owner(grad_parts.reshape(1, 2, 8, 64, COLS))
    pieces = lax.all_to_all(pieces, FSDP, 0, 0, tiled=True)
    new_master, new_one, new_two, copies = adamw(pieces, master_weight, moment_one, moment_two)

    kept, sent = split_features(me, layer_inputs)
    by_y = flipped(sent, "yl")
    by_z = flipped(jnp.concatenate([kept[2:4], by_y[2:4]]), "zl")
    near = jnp.concatenate([kept[0:1], by_y[0:1], by_z[0:1], by_z[2:3]])
    far = flipped(jnp.concatenate([kept[1:2], by_y[1:2], by_z[1:2], by_z[3:4]]), "xl")
    features = []
    for half in (near, far):
        across = flipped(half, "xh")
        features.append((half, flipped(half, "c"), across, flipped(across, "c")))
    features = [features[h][f] for f in range(4) for h in range(2)]

    weight = lax.all_to_all(copies, FAR, 0, 0, tiled=True)

    partial = project(me, own, features, weight)
    partial = (partial * 64.0).astype(jnp.float16)
    partial = lax.all_to_all(partial, CUBE, 0, 0, tiled=True)
    fresh = (jnp.sum(partial.astype(jnp.float32), axis=0) * (1.0 / 64.0)).astype(jnp.bfloat16)

    keys = kv_cache[:, :, 0].reshape(ROWS * CACHE, COLS)
    values = kv_cache[:, :, 1].reshape(ROWS * CACHE, COLS)
    context = attend(lengths, fresh, queries, keys, values)
    return (new_master, new_one, new_two, context)


def solution(mesh):
    finer = Mesh(mesh.devices.reshape(4, 2, 2, 4, 2, 2, 2), AXES)
    shard = P(None, SHARD, TP)
    return jax.shard_map(
        on_device,
        mesh=finer,
        in_specs=(
            P(FSDP, None, REP, TP),
            shard,
            shard,
            shard,
            P(SHARD, None, TP),
            P(SHARD, None, TP),
            P(SHARD, None, None, TP),
            P(SHARD),
        ),
        out_specs=(shard, shard, shard, P(SHARD, None, TP)),
        check_vma=False,
    )
```
